128 devices in a mesh: leaf: 4 (over y), dp: 32 (over z, x, core).
Axes of the slice: x: 4, y: 4, z: 4, core: 2. Of those that a mesh axis runs over, the one named last changes fastest.
Arguments:
- bins: int32 [49152, 256], P('dp'), may hold values from 0 to 255
- outcome: float32 [49152], P('dp'), may hold values from -6 to 6
- treatment: int32 [49152], P('dp'), may hold values 0 or 1
- bag: int32 [196608], P(('leaf', 'dp')), parts along dimension 0, may hold values 0 or 1
- block_node: int32 [384], P('dp'), may hold values from 0 to 15, as said below
Outputs:
- hist_sum: float32 [1024, 16, 256], P(('leaf', 'dp')), parts along dimension 0
- hist_count: float32 [1024, 16, 256], P(('leaf', 'dp')), parts along dimension 0
The draws below stay inside these ranges and needn't reach their ends.
There are 4 independent parts, one for each index of `leaf`. The reference program is written for one: setup_inputs(seed, part) draws one part's arguments, and reference() takes and returns one part's arrays. A program takes and returns all parts, laid end to end along the dimension named above; an argument that names none is the same for every part. Nothing has to cross between parts.
Inputs may be any that keep to these rules, and one draw needn't show every extreme that they name: block_node is nondecreasing along the blocks; every node has 1 to 128 blocks, one exactly that many.
All inputs are finite; a program needn't handle non-finite values. No bound on the sum of `treatment` or of `bag` on one device may be relied on, other than what follows from the above.
Results may differ from the reference program's by a relative error of at most 0.0029.
Values may be sent and summed in bfloat16 or wider, within the bound.
No kernel may reach another device: no remote copies, remote signals or barrier semaphores. Data moves between devices by JAX's collectives and lax.ppermute only.
A program may use at most 64 MiB of HBM per device.

```python
import jax
import jax.numpy as jnp
from jax import lax

FEATURES = 256
BINS = 256
NODES = 16
BLK = 128
BLOCKS = 384
ROWS = 49152


def draw_block_node(key, part):
    key = jax.random.fold_in(key, 7)
    largest = BLOCKS // 3
    first_key = jax.random.fold_in(key, 1)
    spread_key = jax.random.fold_in(key, 2)
    first = jax.random.randint(first_key, (), 0, NODES).astype(jnp.int32)
    counts = jnp.ones((NODES,), jnp.int32)
    counts = jnp.where(jnp.arange(NODES, dtype=jnp.int32) == first, jnp.int32(largest), counts)
    extra = BLOCKS - largest - (NODES - 1)

    def one_step(index, current):
        scores = jax.random.permutation(jax.random.fold_in(spread_key, index), NODES).astype(jnp.int32)
        eligible = current < largest
        pick = jnp.argmax(jnp.where(eligible, scores + 1, jnp.int32(0)))
        return current + (jnp.arange(NODES, dtype=jnp.int32) == pick).astype(jnp.int32)
    counts = lax.fori_loop(0, extra, one_step, counts)
    bounds = jnp.cumsum(counts).astype(jnp.int32)
    positions = jnp.arange(BLOCKS, dtype=jnp.int32)
    return jnp.sum((positions[:, None] >= bounds[None, :]).astype(jnp.int32), axis=1).astype(jnp.int32)


def with_ends(array, own_key, least, high):
    longest = array.shape.index(max(array.shape))
    spots = []
    for shift in (0, 1):
        where = [jax.random.randint(jax.random.fold_in(own_key, axis), (), 0, length) for axis, length in enumerate(array.shape)]
        where[longest] = (where[longest] + shift) % array.shape[longest]
        spots.append(tuple(where))
    return array.at[spots[0]].set(least).at[spots[1]].set(high)


def block_scale(own_key, shape, cuts, low, high):
    def one(axis_at, parts):
        heights = jax.random.uniform(jax.random.fold_in(jax.random.fold_in(own_key, 6), axis_at), (parts,), jnp.float32, low / len(cuts), high / len(cuts))
        return jnp.repeat(jnp.exp(heights), shape[axis_at] // parts).reshape((-1,) + (1,) * (len(shape) - axis_at - 1))

    gain = one(*cuts[0])
    for cut in cuts[1:]:
        gain = gain * one(*cut)
    return gain


def bell_draw(stream_key, dims, scale, limit, cuts=(), held_as=jnp.bfloat16):
    entries = jax.random.normal(stream_key, dims, jnp.float32) * scale
    if len(cuts) > 0:
        entries = block_scale(stream_key, dims, cuts, -0.22, 0.18) * entries
    return jnp.clip(entries, min=-limit, max=limit).astype(held_as)


def setup_inputs(seed: int = 0, part: int = 0) -> dict:
    splits = jax.random.split(jax.random.key(seed), 6)
    part_keys = jax.random.split(jax.random.fold_in(splits[5], part), 6)
    bins = with_ends(jax.random.randint(splits[0], (ROWS, FEATURES), 0, BINS), jax.random.fold_in(splits[0], 1), 0, BINS - 1).astype(jnp.int32)
    outcome = bell_draw(splits[1], (ROWS,), 1.0, 6.0, ((0, 32),), jnp.float32)
    treatment = with_ends((jax.random.randint(splits[2], (ROWS,), 0, 2) < 1).astype(jnp.int32), jax.random.fold_in(splits[2], 1), 0, 1)
    bag = with_ends((jax.random.randint(part_keys[3], (ROWS,), 0, 2) < 1).astype(jnp.int32), jax.random.fold_in(part_keys[3], 1), 0, 1)
    block_node = draw_block_node(jax.random.fold_in(splits[5], 71), part)
    return dict(bins=bins, outcome=outcome, treatment=treatment, bag=bag, block_node=block_node)


def node_params(moments):
    count_n = moments[:, 0]
    sum_w = moments[:, 1]
    sum_y = moments[:, 2]
    sum_wy = moments[:, 3]
    shrunk = count_n + 1.0
    wbar = sum_w / shrunk
    ybar = sum_y / shrunk
    cov = sum_wy - wbar * sum_y - ybar * sum_w + count_n * wbar * ybar
    spread = sum_w - 2.0 * wbar * sum_w + count_n * wbar * wbar + 1.0
    effect = cov / spread
    return jnp.stack([wbar, ybar, effect, shrunk / spread], 1)


def reference(bins, outcome, treatment, bag, block_node):
    node_rows = jnp.repeat(block_node, BLK)
    node_hot = (node_rows[:, None] == jnp.arange(NODES, dtype=jnp.int32)[None, :]).astype(jnp.float32)
    weight = treatment.astype(jnp.float32)
    taken = bag.astype(jnp.float32)
    stats = jnp.stack([taken, taken * weight, taken * outcome, taken * weight * outcome], 1)
    moments = jnp.dot(node_hot.T, stats, precision=lax.Precision.HIGHEST)
    params = node_params(moments)
    row_params = params[node_rows]
    centred = weight - row_params[:, 0]
    rho = taken * centred * ((outcome - row_params[:, 1]) - centred * row_params[:, 2]) * row_params[:, 3]
    rho_low = lax.optimization_barrier(rho.astype(jnp.bfloat16)).astype(jnp.float32)
    index_all = (node_rows[:, None] * BINS + bins).astype(jnp.int32)

    def one_feature(column):
        sums = jax.ops.segment_sum(rho_low, column, num_segments=NODES * BINS)
        counts = jax.ops.segment_sum(taken, column, num_segments=NODES * BINS)
        return sums, counts

    sums, counts = lax.map(one_feature, index_all.T)
    return sums.reshape(FEATURES, NODES, BINS), counts.reshape(FEATURES, NODES, BINS)
```

```python
import functools

import jax
import jax.numpy as jnp
from jax import lax
from jax.experimental import pallas as pl
from jax.experimental.pallas import tpu as pltpu
from jax.sharding import PartitionSpec as P

BINS = 256
NODES = 16
LANES = 128
SLOTS = 16
F32 = jnp.float32
BF16 = jnp.bfloat16
I32 = jnp.int32
I16 = jnp.int16
Y_SCALE = float(2**28)


def pack_kernel(bins_ref, y_ref, w_ref, b_ref, node_ref, out_ref):
    dests = out_ref.shape[0]
    blocks = y_ref.shape[0]
    half = blocks // 2
    for t in range(half):
        low = bins_ref[pl.ds(LANES * t, LANES), :]
        high = bins_ref[pl.ds(LANES * (t + half), LANES), :]
        packed = jnp.bitwise_or(low, lax.shift_left(high, 16)).T
        out_ref[:, pl.ds(8 * t, 8), :] = packed.reshape(dests, 8, LANES)
    base = 8 * half
    fixed = jnp.round(y_ref[...] * Y_SCALE).astype(I32)
    flags = jnp.bitwise_or(w_ref[...], lax.shift_left(b_ref[...], 16))
    tail = jnp.concatenate(
        [
            fixed,
            node_ref[...],
            jnp.zeros((SLOTS - blocks - 1, LANES), I32),
            flags,
            jnp.zeros((SLOTS - blocks, LANES), I32),
        ],
        axis=0,
    )
    out_ref[:, pl.ds(base, 2 * SLOTS), :] = jnp.broadcast_to(tail[None], (dests,) + tail.shape)


def split3(x):
    high = x.astype(BF16)
    rest = x - high.astype(F32)
    mid = rest.astype(BF16)
    low = (rest - mid.astype(F32)).astype(BF16)
    return high, mid, low


def hist_kernel(node_smem, recv_ref, sum_ref, cnt_ref, rho_ref, bag_ref, acc_ref, *, blocks):
    sources = recv_ref.shape[0]
    half = blocks // 2
    base = 8 * half
    rows = sources * SLOTS

    first = recv_ref[:, pl.ds(base, SLOTS), :]
    flags = recv_ref[:, pl.ds(base + SLOTS, SLOTS), :].reshape(rows, LANES)
    y = first.reshape(rows, LANES).astype(F32) * (1.0 / Y_SCALE)
    w = jnp.bitwise_and(flags, 0xFFFF).astype(F32)
    b = lax.shift_right_logical(flags, 16).astype(F32)
    sub = lax.broadcasted_iota(I32, (sources, SLOTS, LANES), 1)
    lane = lax.broadcasted_iota(I32, (sources, SLOTS, LANES), 2)
    node_row = jnp.broadcast_to(first[:, blocks : blocks + 1, :], first.shape).astype(F32)
    node_col = jnp.sum(jnp.where(sub == lane, node_row, 0.0), axis=2, keepdims=True)
    node_col = node_col.reshape(rows, 1)
    lanes = lax.broadcasted_iota(I32, (rows, LANES), 1)
    wanted = jnp.where(lanes < 3 * NODES, jnp.bitwise_and(lanes, NODES - 1), -1).astype(F32)
    hot3 = (jnp.broadcast_to(node_col, (rows, LANES)) == wanted).astype(F32)
    hot_t = hot3.T.astype(BF16)[:NODES]
    bw = b * w
    stats = jnp.concatenate(
        [b.astype(BF16), bw.astype(BF16), *split3(b * y), *split3(bw * y)], axis=1
    )
    sums = jnp.dot(hot_t, stats, preferred_element_type=F32)

    def total(first_part, parts):
        out = sums[:, LANES * first_part : LANES * (first_part + 1)]
        for p in range(1, parts):
            out = out + sums[:, LANES * (first_part + p) : LANES * (first_part + p + 1)]
        return jnp.sum(out, axis=1, keepdims=True)

    count_n = total(0, 1)
    sum_w = total(1, 1)
    sum_y = total(2, 3)
    sum_wy = total(5, 3)
    shrunk = count_n + 1.0
    wbar = sum_w / shrunk
    ybar = sum_y / shrunk
    cov = sum_wy - wbar * sum_y - ybar * sum_w + count_n * wbar * ybar
    spread = sum_w - 2.0 * wbar * sum_w + count_n * wbar * wbar + 1.0
    effect = cov / spread
    scale = shrunk / spread
    params = jnp.concatenate(
        [jnp.broadcast_to(p, (NODES, LANES)) for p in (wbar, ybar, effect, scale)], axis=1
    )
    params = jnp.concatenate(
        [*split3(params), jnp.zeros((LANES - 3 * NODES, 4 * LANES), BF16)], axis=0
    )
    spread_out = jnp.dot(hot3.astype(BF16), params, preferred_element_type=F32)
    r_wbar, r_ybar, r_effect, r_scale = [
        spread_out[:, LANES * p : LANES * (p + 1)] for p in range(4)
    ]
    centred = w - r_wbar
    rho_ref[...] = b * centred * ((y - r_ybar) - centred * r_effect) * r_scale
    bag_ref[...] = b

    acc_ref[...] = jnp.zeros_like(acc_ref)
    iota_hi = jnp.bitwise_and(lax.broadcasted_iota(I32, (16, LANES), 0), 7).astype(I16)
    iota_lo = lax.broadcasted_iota(I32, (32, LANES), 0).astype(I16)
    lane_group = lax.shift_right_logical(lax.broadcasted_iota(I32, (16, LANES), 1), 5)
    one = jnp.ones((32, LANES), BF16)
    zero_lo = jnp.zeros((32, LANES), BF16)
    zero_hi = jnp.zeros((16, LANES), BF16)

    def one_source(s, carry):
        for k in range(blocks):
            tile = recv_ref[s, pl.ds(8 * (k % half), 8), :]
            if k < half:
                tile = jnp.bitwise_and(tile, 0xFFFF)
            else:
                tile = lax.shift_right_logical(tile, 16)
            hi = lax.shift_right_logical(tile, 5)
            lo = jnp.bitwise_and(tile, 31)
            row = s * SLOTS + k
            vals = jnp.concatenate(
                [
                    jnp.broadcast_to(rho_ref[pl.ds(row, 1), :], (8, LANES)),
                    jnp.broadcast_to(bag_ref[pl.ds(row, 1), :], (8, LANES)),
                ],
                axis=0,
            ).astype(BF16)
            node = node_smem[s, k]
            for q in range(2):
                left, right = [], []
                for f in range(4 * q, 4 * q + 4):
                    hi_f = jnp.broadcast_to(hi[f : f + 1], (16, LANES)).astype(I16)
                    lo_f = jnp.broadcast_to(lo[f : f + 1], (32, LANES)).astype(I16)
                    left.append(jnp.where(hi_f == iota_hi, vals, zero_hi))
                    right.append(jnp.where(lo_f == iota_lo, one, zero_lo))
                prod = lax.dot_general(
                    jnp.concatenate(left, axis=0),
                    jnp.concatenate(right, axis=0),
                    (((1,), (1,)), ((), ())),
                    preferred_element_type=F32,
                )
                merged = prod[0:16]
                for i in range(1, 4):
                    merged = jnp.where(lane_group == i, prod[16 * i : 16 * i + 16], merged)
                acc_ref[node, pl.ds(16 * q, 16), :] += merged
        return carry

    lax.fori_loop(0, sources, one_source, 0)

    for v, out_ref in enumerate((sum_ref, cnt_ref)):
        for q in range(2):
            for c in range(2):
                pieces = [acc_ref[:, 16 * q + 8 * v + 4 * c + g, :] for g in range(4)]
                for i in range(4):
                    out = None
                    for g in range(4):
                        shift = (32 * (g - i)) % LANES
                        moved = pltpu.roll(pieces[g], shift, 1) if shift else pieces[g]
                        out = moved if out is None else jnp.where(lane_group == g, moved, out)
                    out_ref[4 * q + i, :, pl.ds(LANES * c, LANES)] = out


def shards(bins, outcome, treatment, bag, block_node):
    blocks = block_node.shape[0]
    dests = lax.axis_size("dp")
    own = bins.shape[1] // dests
    height = 8 * (blocks // 2) + 2 * SLOTS
    node_row = jnp.pad(block_node, (0, LANES - blocks)).reshape(1, LANES)
    packed = pl.pallas_call(
        pack_kernel,
        out_shape=jax.ShapeDtypeStruct((dests, height, LANES), I32),
        compiler_params=pltpu.CompilerParams(vmem_limit_bytes=32 * 2**20),
        name="pack",
    )(
        bins,
        outcome.reshape(blocks, LANES),
        treatment.reshape(blocks, LANES),
        bag.reshape(blocks, LANES),
        node_row,
    )
    recv = lax.all_to_all(packed, "dp", 0, 0, tiled=True)
    nodes = recv[:, 8 * (blocks // 2) + blocks, :blocks]
    out = jax.ShapeDtypeStruct((own, NODES, BINS), F32)
    vmem = pl.BlockSpec(memory_space=pltpu.VMEM)
    return pl.pallas_call(
        functools.partial(hist_kernel, blocks=blocks),
        out_shape=(out, out),
        in_specs=[pl.BlockSpec(memory_space=pltpu.SMEM), vmem],
        out_specs=(vmem, vmem),
        scratch_shapes=[
            pltpu.VMEM((dests * SLOTS, LANES), F32),
            pltpu.VMEM((dests * SLOTS, LANES), F32),
            pltpu.VMEM((NODES, 32, LANES), F32),
        ],
        compiler_params=pltpu.CompilerParams(vmem_limit_bytes=32 * 2**20),
        name="hist",
    )(nodes, recv)


def solution(mesh):
    return jax.shard_map(
        shards,
        mesh=mesh,
        in_specs=(P("dp", None), P("dp"), P("dp"), P(("leaf", "dp")), P("dp")),
        out_specs=(P(("leaf", "dp"), None, None), P(("leaf", "dp"), None, None)),
        check_vma=False,
    )
```

```python
import functools

import jax
import jax.numpy as jnp
from jax import lax
from jax.experimental import pallas as pl
from jax.experimental.pallas import tpu as pltpu
from jax.sharding import PartitionSpec as P

BINS = 256
NODES = 16
LANES = 128
SLOTS = 16
F32 = jnp.float32
BF16 = jnp.bfloat16
I32 = jnp.int32
I16 = jnp.int16
Y_SCALE = float(2**28)


def pack_kernel(bins_ref, y_ref, w_ref, b_ref, node_ref, out_ref):
    dests = out_ref.shape[0]
    blocks = y_ref.shape[0]
    half = blocks // 2
    for t in range(half):
        low = bins_ref[pl.ds(LANES * t, LANES), :]
        high = bins_ref[pl.ds(LANES * (t + half), LANES), :]
        packed = jnp.bitwise_or(low, lax.shift_left(high, 16)).T
        out_ref[:, pl.ds(8 * t, 8), :] = packed.reshape(dests, 8, LANES)
    base = 8 * half
    fixed = jnp.round(y_ref[...] * Y_SCALE).astype(I32)
    flags = jnp.bitwise_or(w_ref[...], lax.shift_left(b_ref[...], 16))
    tail = jnp.concatenate(
        [
            fixed,
            node_ref[...],
            jnp.zeros((SLOTS - blocks - 1, LANES), I32),
            flags,
            jnp.zeros((SLOTS - blocks, LANES), I32),
        ],
        axis=0,
    )
    out_ref[:, pl.ds(base, 2 * SLOTS), :] = jnp.broadcast_to(tail[None], (dests,) + tail.shape)


def split3(x):
    high = x.astype(BF16)
    rest = x - high.astype(F32)
    mid = rest.astype(BF16)
    low = (rest - mid.astype(F32)).astype(BF16)
    return high, mid, low


def hist_kernel(node_smem, recv_ref, sum_ref, cnt_ref, rho_ref, bag_ref, acc_ref, extra_smem, *, blocks):
    sources = recv_ref.shape[0]
    half = blocks // 2
    base = 8 * half
    rows = sources * SLOTS

    first = recv_ref[:, pl.ds(base, SLOTS), :]
    flags = recv_ref[:, pl.ds(base + SLOTS, SLOTS), :].reshape(rows, LANES)
    y = first.reshape(rows, LANES).astype(F32) * (1.0 / Y_SCALE)
    w = jnp.bitwise_and(flags, 0xFFFF).astype(F32)
    b = lax.shift_right_logical(flags, 16).astype(F32)
    sub = lax.broadcasted_iota(I32, (sources, SLOTS, LANES), 1)
    lane = lax.broadcasted_iota(I32, (sources, SLOTS, LANES), 2)
    node_row = jnp.broadcast_to(first[:, blocks : blocks + 1, :], first.shape).astype(F32)
    node_col = jnp.sum(jnp.where(sub == lane, node_row, 0.0), axis=2, keepdims=True)
    node_col = node_col.reshape(rows, 1)
    lanes = lax.broadcasted_iota(I32, (rows, LANES), 1)
    wanted = jnp.where(lanes < 3 * NODES, jnp.bitwise_and(lanes, NODES - 1), -1).astype(F32)
    hot3 = (jnp.broadcast_to(node_col, (rows, LANES)) == wanted).astype(F32)
    hot_t = hot3.T.astype(BF16)[:NODES]
    bw = b * w
    stats = jnp.concatenate(
        [b.astype(BF16), bw.astype(BF16), *split3(b * y), *split3(bw * y)], axis=1
    )
    sums = jnp.dot(hot_t, stats, preferred_element_type=F32)

    def total(first_part, parts):
        out = sums[:, LANES * first_part : LANES * (first_part + 1)]
        for p in range(1, parts):
            out = out + sums[:, LANES * (first_part + p) : LANES * (first_part + p + 1)]
        return jnp.sum(out, axis=1, keepdims=True)

    count_n = total(0, 1)
    sum_w = total(1, 1)
    sum_y = total(2, 3)
    sum_wy = total(5, 3)
    shrunk = count_n + 1.0
    wbar = sum_w / shrunk
    ybar = sum_y / shrunk
    cov = sum_wy - wbar * sum_y - ybar * sum_w + count_n * wbar * ybar
    spread = sum_w - 2.0 * wbar * sum_w + count_n * wbar * wbar + 1.0
    effect = cov / spread
    scale = shrunk / spread
    params = jnp.concatenate(
        [jnp.broadcast_to(p, (NODES, LANES)) for p in (wbar, ybar, effect, scale)], axis=1
    )
    params = jnp.concatenate(
        [*split3(params), jnp.zeros((LANES - 3 * NODES, 4 * LANES), BF16)], axis=0
    )
    spread_out = jnp.dot(hot3.astype(BF16), params, preferred_element_type=F32)
    r_wbar, r_ybar, r_effect, r_scale = [
        spread_out[:, LANES * p : LANES * (p + 1)] for p in range(4)
    ]
    centred = w - r_wbar
    rho_ref[...] = b * centred * ((y - r_ybar) - centred * r_effect) * r_scale
    bag_ref[...] = b

    acc_ref[...] = jnp.zeros_like(acc_ref)
    iota_hi = jnp.bitwise_and(lax.broadcasted_iota(I32, (16, LANES), 0), 7).astype(I16)
    iota_lo = lax.broadcasted_iota(I32, (32, LANES), 0).astype(I16)
    lane_group = lax.shift_right_logical(lax.broadcasted_iota(I32, (16, LANES), 1), 5)
    one = jnp.ones((32, LANES), BF16)
    zero_lo = jnp.zeros((32, LANES), BF16)
    zero_hi = jnp.zeros((16, LANES), BF16)

    group = 4 if blocks % 4 == 0 else 1

    def add_group(s, start, target):
        lefts, rights = ([], []), ([], [])
        for n in range(group):
            k = start + n
            if isinstance(k, int):
                tile = recv_ref[s, pl.ds(8 * (k % half), 8), :]
                if k < half:
                    tile = jnp.bitwise_and(tile, 0xFFFF)
                else:
                    tile = lax.shift_right_logical(tile, 16)
            else:
                upper = (k >= half).astype(I32)
                tile = recv_ref[s, pl.ds(pl.multiple_of(8 * (k - half * upper), 8), 8), :]
                tile = jnp.bitwise_and(lax.shift_right_logical(tile, jnp.full(tile.shape, 16 * upper)), 0xFFFF)
            hi = lax.shift_right_logical(tile, 5)
            lo = jnp.bitwise_and(tile, 31)
            row = s * SLOTS + k
            keep = (node_smem[s, k] == target).astype(F32)
            vals = jnp.concatenate(
                [
                    jnp.broadcast_to(rho_ref[pl.ds(row, 1), :] * keep, (8, LANES)),
                    jnp.broadcast_to(bag_ref[pl.ds(row, 1), :] * keep, (8, LANES)),
                ],
                axis=0,
            ).astype(BF16)
            for q in range(2):
                left, right = [], []
                for f in range(4 * q, 4 * q + 4):
                    hi_f = jnp.broadcast_to(hi[f : f + 1], (16, LANES)).astype(I16)
                    lo_f = jnp.broadcast_to(lo[f : f + 1], (32, LANES)).astype(I16)
                    left.append(jnp.where(hi_f == iota_hi, vals, zero_hi))
                    right.append(jnp.where(lo_f == iota_lo, one, zero_lo))
                lefts[q].append(jnp.concatenate(left, axis=0))
                rights[q].append(jnp.concatenate(right, axis=0))
        for q in range(2):
            prod = lax.dot_general(
                jnp.concatenate(lefts[q], axis=1),
                jnp.concatenate(rights[q], axis=1),
                (((1,), (1,)), ((), ())),
                preferred_element_type=F32,
            )
            merged = prod[0:16]
            for i in range(1, 4):
                merged = jnp.where(lane_group == i, prod[16 * i : 16 * i + 16], merged)
            acc_ref[target, pl.ds(16 * q, 16), :] += merged

    def one_source(s, found):
        for start in range(0, blocks, group):
            add_group(s, start, node_smem[s, start])
            for k in range(start + 1, start + group):
                extra_smem[found] = (s * blocks + start) * NODES + node_smem[s, k]
                found = found + (node_smem[s, k] != node_smem[s, k - 1]).astype(I32)
        return found

    found = lax.fori_loop(0, sources, one_source, jnp.int32(0), unroll=4)

    def one_extra(e, carry):
        code = extra_smem[e]
        place = lax.shift_right_logical(code, 4)
        s = lax.div(place, blocks)
        add_group(s, lax.rem(place, blocks), jnp.bitwise_and(code, NODES - 1))
        return carry

    lax.fori_loop(0, found, one_extra, 0)

    for v, out_ref in enumerate((sum_ref, cnt_ref)):
        for q in range(2):
            for c in range(2):
                pieces = [acc_ref[:, 16 * q + 8 * v + 4 * c + g, :] for g in range(4)]
                for i in range(4):
                    out = None
                    for g in range(4):
                        shift = (32 * (g - i)) % LANES
                        moved = pltpu.roll(pieces[g], shift, 1) if shift else pieces[g]
                        out = moved if out is None else jnp.where(lane_group == g, moved, out)
                    out_ref[4 * q + i, :, pl.ds(LANES * c, LANES)] = out


def shards(bins, outcome, treatment, bag, block_node):
    blocks = block_node.shape[0]
    dests = lax.axis_size("dp")
    own = bins.shape[1] // dests
    height = 8 * (blocks // 2) + 2 * SLOTS
    node_row = jnp.pad(block_node, (0, LANES - blocks)).reshape(1, LANES)
    packed = pl.pallas_call(
        pack_kernel,
        out_shape=jax.ShapeDtypeStruct((dests, height, LANES), I32),
        compiler_params=pltpu.CompilerParams(vmem_limit_bytes=32 * 2**20),
        name="pack",
    )(
        bins,
        outcome.reshape(blocks, LANES),
        treatment.reshape(blocks, LANES),
        bag.reshape(blocks, LANES),
        node_row,
    )
    recv = lax.all_to_all(packed, "dp", 0, 0, tiled=True)
    nodes = recv[:, 8 * (blocks // 2) + blocks, :blocks]
    out = jax.ShapeDtypeStruct((own, NODES, BINS), F32)
    vmem = pl.BlockSpec(memory_space=pltpu.VMEM)
    return pl.pallas_call(
        functools.partial(hist_kernel, blocks=blocks),
        out_shape=(out, out),
        in_specs=[pl.BlockSpec(memory_space=pltpu.SMEM), vmem],
        out_specs=(vmem, vmem),
        scratch_shapes=[
            pltpu.VMEM((dests * SLOTS, LANES), F32),
            pltpu.VMEM((dests * SLOTS, LANES), F32),
            pltpu.VMEM((NODES, 32, LANES), F32),
            pltpu.SMEM((dests * blocks,), I32),
        ],
        compiler_params=pltpu.CompilerParams(vmem_limit_bytes=32 * 2**20),
        name="hist",
    )(nodes, recv)


def solution(mesh):
    return jax.shard_map(
        shards,
        mesh=mesh,
        in_specs=(P("dp", None), P("dp"), P("dp"), P(("leaf", "dp")), P("dp")),
        out_specs=(P(("leaf", "dp"), None, None), P(("leaf", "dp"), None, None)),
        check_vma=False,
    )
```

```python
import functools

import jax
import jax.numpy as jnp
from jax import lax
from jax.experimental import pallas as pl
from jax.experimental.pallas import tpu as pltpu
from jax.sharding import PartitionSpec as P

BINS = 256
NODES = 16
LANES = 128
SLOTS = 16
F32 = jnp.float32
BF16 = jnp.bfloat16
I32 = jnp.int32
I16 = jnp.int16
Y_SCALE = float(2**28)


def pack_kernel(
    bins_hbm, y_hbm, w_hbm, b_hbm, node_hbm, out_ref, bins_ref, y_ref, w_ref, b_ref, node_smem, sems
):
    copies = [
        pltpu.make_async_copy(src, dst, sems.at[n])
        for n, (src, dst) in enumerate(
            (
                (bins_hbm, bins_ref),
                (y_hbm, y_ref),
                (w_hbm, w_ref),
                (b_hbm, b_ref),
                (node_hbm, node_smem),
            )
        )
    ]
    for copy in copies:
        copy.start()
    dests = out_ref.shape[0]
    blocks = y_ref.shape[0]
    half = blocks // 2
    base = 8 * half
    for copy in copies[1:]:
        copy.wait()
    fixed = jnp.round(y_ref[...] * Y_SCALE).astype(I32)
    flags = jnp.bitwise_or(w_ref[...], lax.shift_left(b_ref[...], 16))
    lane = lax.broadcasted_iota(I32, (1, LANES), 1)
    nodes = jnp.zeros((1, LANES), I32)
    for k in range(blocks):
        nodes = jnp.where(lane == k, node_smem[k], nodes)
    tail = jnp.concatenate(
        [
            fixed,
            nodes,
            jnp.zeros((SLOTS - blocks - 1, LANES), I32),
            flags,
            jnp.zeros((SLOTS - blocks, LANES), I32),
        ],
        axis=0,
    )
    out_ref[:, pl.ds(base, 2 * SLOTS), :] = jnp.broadcast_to(tail[None], (dests,) + tail.shape)
    copies[0].wait()
    for t in range(half):
        low = bins_ref[pl.ds(LANES * t, LANES), :]
        high = bins_ref[pl.ds(LANES * (t + half), LANES), :]
        packed = jnp.bitwise_or(low, lax.shift_left(high, 16)).T
        out_ref[:, pl.ds(8 * t, 8), :] = packed.reshape(dests, 8, LANES)


def split3(x):
    high = x.astype(BF16)
    rest = x - high.astype(F32)
    mid = rest.astype(BF16)
    low = (rest - mid.astype(F32)).astype(BF16)
    return high, mid, low


def hist_kernel(node_smem, recv_ref, sum_ref, cnt_ref, rho_ref, bag_ref, acc_ref, extra_smem, *, blocks):
    sources = recv_ref.shape[0]
    half = blocks // 2
    base = 8 * half
    rows = sources * SLOTS

    first = recv_ref[:, pl.ds(base, SLOTS), :]
    flags = recv_ref[:, pl.ds(base + SLOTS, SLOTS), :].reshape(rows, LANES)
    y = first.reshape(rows, LANES).astype(F32) * (1.0 / Y_SCALE)
    w = jnp.bitwise_and(flags, 0xFFFF).astype(F32)
    b = lax.shift_right_logical(flags, 16).astype(F32)
    sub = lax.broadcasted_iota(I32, (sources, SLOTS, LANES), 1)
    lane = lax.broadcasted_iota(I32, (sources, SLOTS, LANES), 2)
    node_row = jnp.broadcast_to(first[:, blocks : blocks + 1, :], first.shape).astype(F32)
    node_col = jnp.sum(jnp.where(sub == lane, node_row, 0.0), axis=2, keepdims=True)
    node_col = node_col.reshape(rows, 1)
    lanes = lax.broadcasted_iota(I32, (rows, LANES), 1)
    wanted = jnp.where(lanes < 3 * NODES, jnp.bitwise_and(lanes, NODES - 1), -1).astype(F32)
    hot3 = (jnp.broadcast_to(node_col, (rows, LANES)) == wanted).astype(F32)
    hot_t = hot3.T.astype(BF16)[:NODES]
    bw = b * w
    stats = jnp.concatenate(
        [b.astype(BF16), bw.astype(BF16), *split3(b * y), *split3(bw * y)], axis=1
    )
    sums = jnp.dot(hot_t, stats, preferred_element_type=F32)

    def total(first_part, parts):
        out = sums[:, LANES * first_part : LANES * (first_part + 1)]
        for p in range(1, parts):
            out = out + sums[:, LANES * (first_part + p) : LANES * (first_part + p + 1)]
        return jnp.sum(out, axis=1, keepdims=True)

    count_n = total(0, 1)
    sum_w = total(1, 1)
    sum_y = total(2, 3)
    sum_wy = total(5, 3)
    shrunk = count_n + 1.0
    wbar = sum_w / shrunk
    ybar = sum_y / shrunk
    cov = sum_wy - wbar * sum_y - ybar * sum_w + count_n * wbar * ybar
    spread = sum_w - 2.0 * wbar * sum_w + count_n * wbar * wbar + 1.0
    effect = cov / spread
    scale = shrunk / spread
    params = jnp.concatenate(
        [jnp.broadcast_to(p, (NODES, LANES)) for p in (wbar, ybar, effect, scale)], axis=1
    )
    params = jnp.concatenate(
        [*split3(params), jnp.zeros((LANES - 3 * NODES, 4 * LANES), BF16)], axis=0
    )
    spread_out = jnp.dot(hot3.astype(BF16), params, preferred_element_type=F32)
    r_wbar, r_ybar, r_effect, r_scale = [
        spread_out[:, LANES * p : LANES * (p + 1)] for p in range(4)
    ]
    centred = w - r_wbar
    rho_ref[...] = b * centred * ((y - r_ybar) - centred * r_effect) * r_scale
    bag_ref[...] = b

    acc_ref[...] = jnp.zeros_like(acc_ref)
    iota_bin = lax.broadcasted_iota(I32, (16, LANES), 0).astype(I16)
    lane_group = lax.shift_right_logical(lax.broadcasted_iota(I32, (NODES, LANES), 1), 4)
    merge_group = lax.shift_right_logical(lax.broadcasted_iota(I32, (32, LANES), 1), 4)
    one = jnp.ones((16, LANES), BF16)
    zero = jnp.zeros((16, LANES), BF16)
    group = 4 if blocks % 4 == 0 else 1

    def add_group(s, start, target):
        lefts, rights = [], []
        for n in range(group):
            k = start + n
            if isinstance(k, int):
                tile = recv_ref[s, pl.ds(8 * (k % half), 8), :]
                if k < half:
                    tile = jnp.bitwise_and(tile, 0xFFFF)
                else:
                    tile = lax.shift_right_logical(tile, 16)
            else:
                upper = (k >= half).astype(I32)
                tile = recv_ref[s, pl.ds(pl.multiple_of(8 * (k - half * upper), 8), 8), :]
                tile = jnp.bitwise_and(lax.shift_right_logical(tile, jnp.full(tile.shape, 16 * upper)), 0xFFFF)
            hi = lax.shift_right_logical(tile, 4)
            lo = jnp.bitwise_and(tile, 15)
            row = s * SLOTS + k
            keep = (node_smem[s, k] == target).astype(F32)
            rho = jnp.broadcast_to(rho_ref[pl.ds(row, 1), :] * keep, (16, LANES)).astype(BF16)
            bag = jnp.broadcast_to(bag_ref[pl.ds(row, 1), :] * keep, (16, LANES)).astype(BF16)
            left, right = [], []
            for f in range(8):
                hot = jnp.broadcast_to(hi[f : f + 1], (16, LANES)).astype(I16) == iota_bin
                left += [jnp.where(hot, rho, zero), jnp.where(hot, bag, zero)]
                hot = jnp.broadcast_to(lo[f : f + 1], (16, LANES)).astype(I16) == iota_bin
                right.append(jnp.where(hot, one, zero))
            lefts.append(jnp.concatenate(left, axis=0))
            rights.append(jnp.concatenate(right, axis=0))
        prod = lax.dot_general(
            jnp.concatenate(lefts, axis=1),
            jnp.concatenate(rights, axis=1),
            (((1,), (1,)), ((), ())),
            preferred_element_type=F32,
        )
        merged = prod[0:32]
        for f in range(1, 8):
            merged = jnp.where(merge_group == f, prod[32 * f : 32 * f + 32], merged)
        return merged

    def one_source(s, found):
        pending = []
        for start in range(0, blocks, group):
            pending.append((node_smem[s, start], add_group(s, start, node_smem[s, start])))
            for k in range(start + 1, start + group):
                extra_smem[found] = (s * blocks + start) * NODES + node_smem[s, k]
                found = found + (node_smem[s, k] != node_smem[s, k - 1]).astype(I32)
        for target, merged in pending:
            acc_ref[target] += merged
        return found

    found = lax.fori_loop(0, sources, one_source, jnp.int32(0), unroll=8)

    def one_extra(e, carry):
        code = extra_smem[e]
        place = lax.shift_right_logical(code, 4)
        s = lax.div(place, blocks)
        target = jnp.bitwise_and(code, NODES - 1)
        acc_ref[target] += add_group(s, lax.rem(place, blocks), target)
        return carry

    lax.fori_loop(0, found, one_extra, 0)

    for v, out_ref in enumerate((sum_ref, cnt_ref)):
        for c in range(2):
            pieces = [acc_ref[:, 16 * v + 8 * c + g, :] for g in range(8)]
            for f in range(8):
                out = None
                for g in range(8):
                    shift = (16 * (g - f)) % LANES
                    moved = pltpu.roll(pieces[g], shift, 1) if shift else pieces[g]
                    out = moved if out is None else jnp.where(lane_group == g, moved, out)
                out_ref[f, :, pl.ds(LANES * c, LANES)] = out


def shards(bins, outcome, treatment, bag, block_node):
    blocks = block_node.shape[0]
    dests = lax.axis_size("dp")
    own = bins.shape[1] // dests
    height = 8 * (blocks // 2) + 2 * SLOTS
    packed = pl.pallas_call(
        pack_kernel,
        out_shape=jax.ShapeDtypeStruct((dests, height, LANES), I32),
        in_specs=[pl.BlockSpec(memory_space=pl.ANY)] * 5,
        out_specs=pl.BlockSpec(memory_space=pltpu.VMEM),
        scratch_shapes=[
            pltpu.VMEM(bins.shape, I32),
            pltpu.VMEM((blocks, LANES), F32),
            pltpu.VMEM((blocks, LANES), I32),
            pltpu.VMEM((blocks, LANES), I32),
            pltpu.SMEM((blocks,), I32),
            pltpu.SemaphoreType.DMA((5,)),
        ],
        compiler_params=pltpu.CompilerParams(vmem_limit_bytes=60 * 2**20),
        name="pack",
    )(
        bins,
        outcome.reshape(blocks, LANES),
        treatment.reshape(blocks, LANES),
        bag.reshape(blocks, LANES),
        block_node,
    )
    recv = lax.all_to_all(packed, "dp", 0, 0, tiled=True)
    nodes = recv[:, 8 * (blocks // 2) + blocks, :blocks]
    out = jax.ShapeDtypeStruct((own, NODES, BINS), F32)
    vmem = pl.BlockSpec(memory_space=pltpu.VMEM)
    return pl.pallas_call(
        functools.partial(hist_kernel, blocks=blocks),
        out_shape=(out, out),
        in_specs=[pl.BlockSpec(memory_space=pltpu.SMEM), vmem],
        out_specs=(vmem, vmem),
        scratch_shapes=[
            pltpu.VMEM((dests * SLOTS, LANES), F32),
            pltpu.VMEM((dests * SLOTS, LANES), F32),
            pltpu.VMEM((NODES, 32, LANES), F32),
            pltpu.SMEM((dests * blocks,), I32),
        ],
        compiler_params=pltpu.CompilerParams(vmem_limit_bytes=32 * 2**20),
        name="hist",
    )(nodes, recv)


def solution(mesh):
    return jax.shard_map(
        shards,
        mesh=mesh,
        in_specs=(P("dp", None), P("dp"), P("dp"), P(("leaf", "dp")), P("dp")),
        out_specs=(P(("leaf", "dp"), None, None), P(("leaf", "dp"), None, None)),
        check_vma=False,
    )
```

```python
import functools

import jax
import jax.numpy as jnp
from jax import lax
from jax.experimental import pallas as pl
from jax.experimental.pallas import tpu as pltpu
from jax.sharding import PartitionSpec as P

BINS = 256
NODES = 16
LANES = 128
SLOTS = 16
F32 = jnp.float32
BF16 = jnp.bfloat16
I32 = jnp.int32
I16 = jnp.int16
Y_SCALE = float(2**28)


def pack_kernel(
    bins_hbm, y_hbm, w_hbm, b_hbm, node_hbm, out_ref, bins_ref, y_ref, w_ref, b_ref, node_smem, sems
):
    copies = [
        pltpu.make_async_copy(src, dst, sems.at[n])
        for n, (src, dst) in enumerate(
            (
                (bins_hbm, bins_ref),
                (y_hbm, y_ref),
                (w_hbm, w_ref),
                (b_hbm, b_ref),
                (node_hbm, node_smem),
            )
        )
    ]
    for copy in copies:
        copy.start()
    dests = out_ref.shape[0]
    blocks = y_ref.shape[0]
    half = blocks // 2
    base = 8 * half
    for copy in copies[1:]:
        copy.wait()
    fixed = jnp.round(y_ref[...] * Y_SCALE).astype(I32)
    flags = jnp.bitwise_or(w_ref[...], lax.shift_left(b_ref[...], 16))
    lane = lax.broadcasted_iota(I32, (1, LANES), 1)
    nodes = jnp.zeros((1, LANES), I32)
    for k in range(blocks):
        nodes = jnp.where(lane == k, node_smem[k], nodes)
    tail = jnp.concatenate(
        [
            fixed,
            nodes,
            jnp.zeros((SLOTS - blocks - 1, LANES), I32),
            flags,
            jnp.zeros((SLOTS - blocks, LANES), I32),
        ],
        axis=0,
    )
    out_ref[:, pl.ds(base, 2 * SLOTS), :] = jnp.broadcast_to(tail[None], (dests,) + tail.shape)
    copies[0].wait()
    for t in range(half):
        low = bins_ref[pl.ds(LANES * t, LANES), :]
        high = bins_ref[pl.ds(LANES * (t + half), LANES), :]
        packed = jnp.bitwise_or(low, lax.shift_left(high, 16)).T
        out_ref[:, pl.ds(8 * t, 8), :] = packed.reshape(dests, 8, LANES)


def split3(x):
    high = x.astype(BF16)
    rest = x - high.astype(F32)
    mid = rest.astype(BF16)
    low = (rest - mid.astype(F32)).astype(BF16)
    return high, mid, low


def hist_kernel(node_smem, recv_ref, sum_ref, cnt_ref, rho_ref, bag_ref, acc_ref, extra_smem, *, blocks):
    sources = recv_ref.shape[0]
    half = blocks // 2
    base = 8 * half
    rows = sources * SLOTS

    first = recv_ref[:, pl.ds(base, SLOTS), :]
    flags = recv_ref[:, pl.ds(base + SLOTS, SLOTS), :].reshape(rows, LANES)
    y = first.reshape(rows, LANES).astype(F32) * (1.0 / Y_SCALE)
    w = jnp.bitwise_and(flags, 0xFFFF).astype(F32)
    b = lax.shift_right_logical(flags, 16).astype(F32)
    sub = lax.broadcasted_iota(I32, (sources, SLOTS, LANES), 1)
    lane = lax.broadcasted_iota(I32, (sources, SLOTS, LANES), 2)
    node_row = jnp.broadcast_to(first[:, blocks : blocks + 1, :], first.shape).astype(F32)
    node_col = jnp.sum(jnp.where(sub == lane, node_row, 0.0), axis=2, keepdims=True)
    node_col = node_col.reshape(rows, 1)
    lanes = lax.broadcasted_iota(I32, (rows, LANES), 1)
    wanted = jnp.where(lanes < 3 * NODES, jnp.bitwise_and(lanes, NODES - 1), -1).astype(F32)
    hot3 = (jnp.broadcast_to(node_col, (rows, LANES)) == wanted).astype(F32)
    hot_t = hot3.T.astype(BF16)[:NODES]
    bw = b * w
    stats = jnp.concatenate(
        [b.astype(BF16), bw.astype(BF16), *split3(b * y), *split3(bw * y)], axis=1
    )
    sums = jnp.dot(hot_t, stats, preferred_element_type=F32)

    def total(first_part, parts):
        out = sums[:, LANES * first_part : LANES * (first_part + 1)]
        for p in range(1, parts):
            out = out + sums[:, LANES * (first_part + p) : LANES * (first_part + p + 1)]
        return jnp.sum(out, axis=1, keepdims=True)

    count_n = total(0, 1)
    sum_w = total(1, 1)
    sum_y = total(2, 3)
    sum_wy = total(5, 3)
    shrunk = count_n + 1.0
    wbar = sum_w / shrunk
    ybar = sum_y / shrunk
    cov = sum_wy - wbar * sum_y - ybar * sum_w + count_n * wbar * ybar
    spread = sum_w - 2.0 * wbar * sum_w + count_n * wbar * wbar + 1.0
    effect = cov / spread
    scale = shrunk / spread
    params = jnp.concatenate(
        [jnp.broadcast_to(p, (NODES, LANES)) for p in (wbar, ybar, effect, scale)], axis=1
    )
    params = jnp.concatenate(
        [*split3(params), jnp.zeros((LANES - 3 * NODES, 4 * LANES), BF16)], axis=0
    )
    spread_out = jnp.dot(hot3.astype(BF16), params, preferred_element_type=F32)
    r_wbar, r_ybar, r_effect, r_scale = [
        spread_out[:, LANES * p : LANES * (p + 1)] for p in range(4)
    ]
    centred = w - r_wbar
    rho_ref[...] = b * centred * ((y - r_ybar) - centred * r_effect) * r_scale
    bag_ref[...] = b

    acc_ref[...] = jnp.zeros_like(acc_ref)
    iota_bin = lax.broadcasted_iota(I32, (16, LANES), 0).astype(I16)
    lane_group = lax.shift_right_logical(lax.broadcasted_iota(I32, (NODES, LANES), 1), 4)
    merge_group = lax.shift_right_logical(lax.broadcasted_iota(I32, (32, LANES), 1), 4)
    one = jnp.ones((16, LANES), BF16)
    zero = jnp.zeros((16, LANES), BF16)
    group = 4 if blocks % 4 == 0 else 1

    def group_sums(s, start, target):
        lefts, rights = [], []
        for n in range(group):
            k = start + n
            if isinstance(k, int):
                tile = recv_ref[s, pl.ds(8 * (k % half), 8), :]
                if k < half:
                    tile = jnp.bitwise_and(tile, 0xFFFF)
                else:
                    tile = lax.shift_right_logical(tile, 16)
            else:
                upper = (k >= half).astype(I32)
                tile = recv_ref[s, pl.ds(pl.multiple_of(8 * (k - half * upper), 8), 8), :]
                tile = jnp.bitwise_and(lax.shift_right_logical(tile, jnp.full(tile.shape, 16 * upper)), 0xFFFF)
            hi = lax.shift_right_logical(tile, 4)
            lo = jnp.bitwise_and(tile, 15)
            row = s * SLOTS + k
            keep = (node_smem[s, k] == target).astype(F32)
            rho = jnp.broadcast_to(rho_ref[pl.ds(row, 1), :] * keep, (16, LANES)).astype(BF16)
            bag = jnp.broadcast_to(bag_ref[pl.ds(row, 1), :] * keep, (16, LANES)).astype(BF16)
            left, right = [], []
            for f in range(8):
                hot = jnp.broadcast_to(hi[f : f + 1], (16, LANES)).astype(I16) == iota_bin
                left += [jnp.where(hot, rho, zero), jnp.where(hot, bag, zero)]
                hot = jnp.broadcast_to(lo[f : f + 1], (16, LANES)).astype(I16) == iota_bin
                right.append(jnp.where(hot, one, zero))
            lefts.append(jnp.concatenate(left, axis=0))
            rights.append(jnp.concatenate(right, axis=0))
        prod = lax.dot_general(
            jnp.concatenate(lefts, axis=1),
            jnp.concatenate(rights, axis=1),
            (((1,), (1,)), ((), ())),
            preferred_element_type=F32,
        )
        merged = prod[0:32]
        for f in range(1, 8):
            merged = jnp.where(merge_group == f, prod[32 * f : 32 * f + 32], merged)
        return merged

    def one_source(s, found):
        pending = []
        for start in range(0, blocks, group):
            pending.append((node_smem[s, start], group_sums(s, start, node_smem[s, start])))
            for k in range(start + 1, start + group):
                extra_smem[found] = (s * blocks + start) * 32 + node_smem[s, k]
                found = found + (node_smem[s, k] != node_smem[s, k - 1]).astype(I32)
        for target, merged in pending:
            acc_ref[target] += merged
        return found

    found = lax.fori_loop(0, sources, one_source, jnp.int32(0), unroll=16)

    batch = 4
    for n in range(batch - 1):
        extra_smem[found + n] = jnp.int32(NODES)

    def some_extras(e, carry):
        pending = []
        for n in range(batch):
            code = extra_smem[batch * e + n]
            target = jnp.bitwise_and(code, 31)
            place = lax.shift_right_logical(code, 5)
            start = lax.rem(place, blocks)
            pending.append((target, group_sums(lax.div(place, blocks), start, target)))
        for target, merged in pending:
            acc_ref[target] += merged
        return carry

    lax.fori_loop(0, lax.div(found + batch - 1, batch), some_extras, 0)

    for v, out_ref in enumerate((sum_ref, cnt_ref)):
        for c in range(2):
            pieces = [acc_ref[:NODES, 16 * v + 8 * c + g, :] for g in range(8)]
            for f in range(8):
                out = None
                for g in range(8):
                    shift = (16 * (g - f)) % LANES
                    moved = pltpu.roll(pieces[g], shift, 1) if shift else pieces[g]
                    out = moved if out is None else jnp.where(lane_group == g, moved, out)
                out_ref[f, :, pl.ds(LANES * c, LANES)] = out


def shards(bins, outcome, treatment, bag, block_node):
    blocks = block_node.shape[0]
    dests = lax.axis_size("dp")
    own = bins.shape[1] // dests
    height = 8 * (blocks // 2) + 2 * SLOTS
    packed = pl.pallas_call(
        pack_kernel,
        out_shape=jax.ShapeDtypeStruct((dests, height, LANES), I32),
        in_specs=[pl.BlockSpec(memory_space=pl.ANY)] * 5,
        out_specs=pl.BlockSpec(memory_space=pltpu.VMEM),
        scratch_shapes=[
            pltpu.VMEM(bins.shape, I32),
            pltpu.VMEM((blocks, LANES), F32),
            pltpu.VMEM((blocks, LANES), I32),
            pltpu.VMEM((blocks, LANES), I32),
            pltpu.SMEM((blocks,), I32),
            pltpu.SemaphoreType.DMA((5,)),
        ],
        compiler_params=pltpu.CompilerParams(vmem_limit_bytes=60 * 2**20),
        name="pack",
    )(
        bins,
        outcome.reshape(blocks, LANES),
        treatment.reshape(blocks, LANES),
        bag.reshape(blocks, LANES),
        block_node,
    )
    recv = lax.all_to_all(packed, "dp", 0, 0, tiled=True)
    nodes = recv[:, 8 * (blocks // 2) + blocks, :blocks]
    out = jax.ShapeDtypeStruct((own, NODES, BINS), F32)
    vmem = pl.BlockSpec(memory_space=pltpu.VMEM)
    return pl.pallas_call(
        functools.partial(hist_kernel, blocks=blocks),
        out_shape=(out, out),
        in_specs=[pl.BlockSpec(memory_space=pltpu.SMEM), vmem],
        out_specs=(vmem, vmem),
        scratch_shapes=[
            pltpu.VMEM((dests * SLOTS, LANES), F32),
            pltpu.VMEM((dests * SLOTS, LANES), F32),
            pltpu.VMEM((NODES + 1, 32, LANES), F32),
            pltpu.SMEM((dests * blocks,), I32),
        ],
        compiler_params=pltpu.CompilerParams(vmem_limit_bytes=32 * 2**20),
        name="hist",
    )(nodes, recv)


def solution(mesh):
    return jax.shard_map(
        shards,
        mesh=mesh,
        in_specs=(P("dp", None), P("dp"), P("dp"), P(("leaf", "dp")), P("dp")),
        out_specs=(P(("leaf", "dp"), None, None), P(("leaf", "dp"), None, None)),
        check_vma=False,
    )
```

```python
import functools

import jax
import jax.numpy as jnp
from jax import lax
from jax.experimental import pallas as pl
from jax.experimental.pallas import tpu as pltpu
from jax.sharding import PartitionSpec as P

BINS = 256
NODES = 16
LANES = 128
SLOTS = 16
F32 = jnp.float32
BF16 = jnp.bfloat16
I32 = jnp.int32
I16 = jnp.int16
Y_SCALE = float(2**20)
TAIL = 24


def pack_kernel(
    bins_hbm, y_hbm, w_hbm, b_hbm, node_hbm, out_ref, bins_ref, y_ref, w_ref, b_ref, node_smem, sems
):
    copies = [
        pltpu.make_async_copy(src, dst, sems.at[n])
        for n, (src, dst) in enumerate(
            (
                (bins_hbm, bins_ref),
                (y_hbm, y_ref),
                (w_hbm, w_ref),
                (b_hbm, b_ref),
                (node_hbm, node_smem),
            )
        )
    ]
    for copy in copies:
        copy.start()
    dests = out_ref.shape[0]
    blocks = y_ref.shape[0]
    half = blocks // 2
    base = 8 * half
    for copy in copies[1:]:
        copy.wait()
    fixed = jnp.bitwise_and(jnp.round(y_ref[...] * Y_SCALE).astype(I32), 0xFFFFFF)
    flags = jnp.bitwise_or(w_ref[...], lax.shift_left(b_ref[...], 16))
    lane = lax.broadcasted_iota(I32, (1, LANES), 1)
    nodes = jnp.zeros((1, LANES), I32)
    for k in range(blocks):
        nodes = jnp.where(lane == k, node_smem[k], nodes)
    last = fixed[11:12]
    top = lax.shift_left(lax.shift_right_logical(last, 16), 24)
    tail = jnp.concatenate(
        [
            fixed[0:3],
            jnp.bitwise_or(fixed[3:4], top),
            fixed[4:8],
            flags[8:12],
            fixed[8:11],
            jnp.bitwise_or(jnp.bitwise_and(last, 0xFFFF), lax.shift_left(nodes, 16)),
            flags[0:8],
        ],
        axis=0,
    )
    out_ref[:, pl.ds(base, TAIL), :] = jnp.broadcast_to(tail[None], (dests,) + tail.shape)
    copies[0].wait()
    for t in range(half):
        low = bins_ref[pl.ds(LANES * t, LANES), :]
        high = bins_ref[pl.ds(LANES * (t + half), LANES), :]
        packed = jnp.bitwise_or(low, lax.shift_left(high, 16)).T
        out_ref[:, pl.ds(8 * t, 8), :] = packed.reshape(dests, 8, LANES)


def split3(x):
    high = x.astype(BF16)
    rest = x - high.astype(F32)
    mid = rest.astype(BF16)
    low = (rest - mid.astype(F32)).astype(BF16)
    return high, mid, low


def hist_kernel(node_smem, recv_ref, sum_ref, cnt_ref, rho_ref, bag_ref, acc_ref, extra_smem, *, blocks):
    sources = recv_ref.shape[0]
    half = blocks // 2
    base = 8 * half
    rows = sources * SLOTS

    part_a, part_b, part_c = [recv_ref[:, pl.ds(base + 8 * p, 8), :] for p in range(3)]
    sub8 = lax.broadcasted_iota(I32, part_b.shape, 1)
    flags = jnp.concatenate([part_c, jnp.where(sub8 < 4, part_b, 0)], axis=1).reshape(rows, LANES)
    upper = pltpu.roll(part_b, 4, 1)
    mixed = jnp.bitwise_or(
        jnp.bitwise_and(upper, 0xFFFF),
        lax.shift_left(lax.shift_right_logical(part_a, 24), 16),
    )
    fixed = jnp.concatenate([part_a, jnp.where(sub8 == 3, mixed, upper)], axis=1)
    fixed = lax.shift_right_arithmetic(lax.shift_left(fixed, 8), 8)
    y = fixed.reshape(rows, LANES).astype(F32) * (1.0 / Y_SCALE)
    w = jnp.bitwise_and(flags, 0xFFFF).astype(F32)
    b = lax.shift_right_logical(flags, 16).astype(F32)
    sub = lax.broadcasted_iota(I32, (sources, SLOTS, LANES), 1)
    lane = lax.broadcasted_iota(I32, (sources, SLOTS, LANES), 2)
    node_row = lax.shift_right_logical(part_b[:, 7:8, :], 16).astype(F32)
    node_row = jnp.broadcast_to(node_row, (sources, SLOTS, LANES))
    node_col = jnp.sum(jnp.where(sub == lane, node_row, 0.0), axis=2, keepdims=True)
    node_col = node_col.reshape(rows, 1)
    lanes = lax.broadcasted_iota(I32, (rows, LANES), 1)
    wanted = jnp.where(lanes < 3 * NODES, jnp.bitwise_and(lanes, NODES - 1), -1).astype(F32)
    hot3 = (jnp.broadcast_to(node_col, (rows, LANES)) == wanted).astype(F32)
    hot_t = hot3.T.astype(BF16)[:NODES]
    bw = b * w
    stats = jnp.concatenate(
        [b.astype(BF16), bw.astype(BF16), *split3(b * y), *split3(bw * y)], axis=1
    )
    sums = jnp.dot(hot_t, stats, preferred_element_type=F32)

    def total(first_part, parts):
        out = sums[:, LANES * first_part : LANES * (first_part + 1)]
        for p in range(1, parts):
            out = out + sums[:, LANES * (first_part + p) : LANES * (first_part + p + 1)]
        return jnp.sum(out, axis=1, keepdims=True)

    count_n = total(0, 1)
    sum_w = total(1, 1)
    sum_y = total(2, 3)
    sum_wy = total(5, 3)
    shrunk = count_n + 1.0
    wbar = sum_w / shrunk
    ybar = sum_y / shrunk
    cov = sum_wy - wbar * sum_y - ybar * sum_w + count_n * wbar * ybar
    spread = sum_w - 2.0 * wbar * sum_w + count_n * wbar * wbar + 1.0
    effect = cov / spread
    scale = shrunk / spread
    params = jnp.concatenate(
        [jnp.broadcast_to(p, (NODES, LANES)) for p in (wbar, ybar, effect, scale)], axis=1
    )
    params = jnp.concatenate(
        [*split3(params), jnp.zeros((LANES - 3 * NODES, 4 * LANES), BF16)], axis=0
    )
    spread_out = jnp.dot(hot3.astype(BF16), params, preferred_element_type=F32)
    r_wbar, r_ybar, r_effect, r_scale = [
        spread_out[:, LANES * p : LANES * (p + 1)] for p in range(4)
    ]
    centred = w - r_wbar
    rho_ref[...] = b * centred * ((y - r_ybar) - centred * r_effect) * r_scale
    bag_ref[...] = b

    acc_ref[...] = jnp.zeros_like(acc_ref)
    iota_bin = lax.broadcasted_iota(I32, (16, LANES), 0).astype(I16)
    lane_group = lax.shift_right_logical(lax.broadcasted_iota(I32, (NODES, LANES), 1), 4)
    merge_group = lax.shift_right_logical(lax.broadcasted_iota(I32, (32, LANES), 1), 4)
    one = jnp.ones((16, LANES), BF16)
    zero = jnp.zeros((16, LANES), BF16)
    group = 4 if blocks % 4 == 0 else 1

    def group_sums(s, start, target):
        lefts, rights = [], []
        for n in range(group):
            k = start + n
            if isinstance(k, int):
                tile = recv_ref[s, pl.ds(8 * (k % half), 8), :]
                if k < half:
                    tile = jnp.bitwise_and(tile, 0xFFFF)
                else:
                    tile = lax.shift_right_logical(tile, 16)
            else:
                upper = (k >= half).astype(I32)
                tile = recv_ref[s, pl.ds(pl.multiple_of(8 * (k - half * upper), 8), 8), :]
                tile = jnp.bitwise_and(lax.shift_right_logical(tile, jnp.full(tile.shape, 16 * upper)), 0xFFFF)
            hi = lax.shift_right_logical(tile, 4)
            lo = jnp.bitwise_and(tile, 15)
            row = s * SLOTS + k
            keep = (node_smem[s, k] == target).astype(F32)
            rho = jnp.broadcast_to(rho_ref[pl.ds(row, 1), :] * keep, (16, LANES)).astype(BF16)
            bag = jnp.broadcast_to(bag_ref[pl.ds(row, 1), :] * keep, (16, LANES)).astype(BF16)
            left, right = [], []
            for f in range(8):
                hot = jnp.broadcast_to(hi[f : f + 1], (16, LANES)).astype(I16) == iota_bin
                left += [jnp.where(hot, rho, zero), jnp.where(hot, bag, zero)]
                hot = jnp.broadcast_to(lo[f : f + 1], (16, LANES)).astype(I16) == iota_bin
                right.append(jnp.where(hot, one, zero))
            lefts.append(jnp.concatenate(left, axis=0))
            rights.append(jnp.concatenate(right, axis=0))
        prod = lax.dot_general(
            jnp.concatenate(lefts, axis=1),
            jnp.concatenate(rights, axis=1),
            (((1,), (1,)), ((), ())),
            preferred_element_type=F32,
        )
        merged = prod[0:32]
        for f in range(1, 8):
            merged = jnp.where(merge_group == f, prod[32 * f : 32 * f + 32], merged)
        return merged

    def one_source(s, found):
        pending = []
        for start in range(0, blocks, group):
            pending.append((node_smem[s, start], group_sums(s, start, node_smem[s, start])))
            for k in range(start + 1, start + group):
                extra_smem[found] = (s * blocks + start) * 32 + node_smem[s, k]
                found = found + (node_smem[s, k] != node_smem[s, k - 1]).astype(I32)
        for target, merged in pending:
            acc_ref[target] += merged
        return found

    found = lax.fori_loop(0, sources, one_source, jnp.int32(0), unroll=16)

    batch = 4
    for n in range(batch - 1):
        extra_smem[found + n] = jnp.int32(NODES)

    def some_extras(e, carry):
        pending = []
        for n in range(batch):
            code = extra_smem[batch * e + n]
            target = jnp.bitwise_and(code, 31)
            place = lax.shift_right_logical(code, 5)
            start = lax.rem(place, blocks)
            pending.append((target, group_sums(lax.div(place, blocks), start, target)))
        for target, merged in pending:
            acc_ref[target] += merged
        return carry

    lax.fori_loop(0, lax.div(found + batch - 1, batch), some_extras, 0)

    for v, out_ref in enumerate((sum_ref, cnt_ref)):
        for c in range(2):
            pieces = [acc_ref[:NODES, 16 * v + 8 * c + g, :] for g in range(8)]
            for f in range(8):
                out = None
                for g in range(8):
                    shift = (16 * (g - f)) % LANES
                    moved = pltpu.roll(pieces[g], shift, 1) if shift else pieces[g]
                    out = moved if out is None else jnp.where(lane_group == g, moved, out)
                out_ref[f, :, pl.ds(LANES * c, LANES)] = out


def shards(bins, outcome, treatment, bag, block_node):
    blocks = block_node.shape[0]
    dests = lax.axis_size("dp")
    own = bins.shape[1] // dests
    base = 8 * (blocks // 2)
    height = base + TAIL
    packed = pl.pallas_call(
        pack_kernel,
        out_shape=jax.ShapeDtypeStruct((dests, height, LANES), I32),
        in_specs=[pl.BlockSpec(memory_space=pl.ANY)] * 5,
        out_specs=pl.BlockSpec(memory_space=pltpu.VMEM),
        scratch_shapes=[
            pltpu.VMEM(bins.shape, I32),
            pltpu.VMEM((blocks, LANES), F32),
            pltpu.VMEM((blocks, LANES), I32),
            pltpu.VMEM((blocks, LANES), I32),
            pltpu.SMEM((blocks,), I32),
            pltpu.SemaphoreType.DMA((5,)),
        ],
        compiler_params=pltpu.CompilerParams(vmem_limit_bytes=60 * 2**20),
        name="pack",
    )(
        bins,
        outcome.reshape(blocks, LANES),
        treatment.reshape(blocks, LANES),
        bag.reshape(blocks, LANES),
        block_node,
    )
    recv = lax.all_to_all(packed, "dp", 0, 0, tiled=True)
    nodes = lax.shift_right_logical(recv[:, base + 15, :blocks], 16)
    out = jax.ShapeDtypeStruct((own, NODES, BINS), F32)
    vmem = pl.BlockSpec(memory_space=pltpu.VMEM)
    return pl.pallas_call(
        functools.partial(hist_kernel, blocks=blocks),
        out_shape=(out, out),
        in_specs=[pl.BlockSpec(memory_space=pltpu.SMEM), vmem],
        out_specs=(vmem, vmem),
        scratch_shapes=[
            pltpu.VMEM((dests * SLOTS, LANES), F32),
            pltpu.VMEM((dests * SLOTS, LANES), F32),
            pltpu.VMEM((NODES + 1, 32, LANES), F32),
            pltpu.SMEM((dests * blocks,), I32),
        ],
        compiler_params=pltpu.CompilerParams(vmem_limit_bytes=32 * 2**20),
        name="hist",
    )(nodes, recv)


def solution(mesh):
    return jax.shard_map(
        shards,
        mesh=mesh,
        in_specs=(P("dp", None), P("dp"), P("dp"), P(("leaf", "dp")), P("dp")),
        out_specs=(P(("leaf", "dp"), None, None), P(("leaf", "dp"), None, None)),
        check_vma=False,
    )
```

```python
import functools

import jax
import jax.numpy as jnp
from jax import lax
from jax.experimental import pallas as pl
from jax.experimental.pallas import tpu as pltpu
from jax.sharding import PartitionSpec as P

BINS = 256
NODES = 16
LANES = 128
SLOTS = 16
F32 = jnp.float32
BF16 = jnp.bfloat16
I32 = jnp.int32
I16 = jnp.int16
Y_SCALE = float(2**20)
TAIL = 24


def pack_kernel(
    bins_hbm, y_hbm, w_hbm, b_hbm, node_hbm, out_ref, bins_ref, y_ref, w_ref, b_ref, node_smem, sems
):
    copies = [
        pltpu.make_async_copy(src, dst, sems.at[n])
        for n, (src, dst) in enumerate(
            (
                (bins_hbm, bins_ref),
                (y_hbm, y_ref),
                (w_hbm, w_ref),
                (b_hbm, b_ref),
                (node_hbm, node_smem),
            )
        )
    ]
    for copy in copies:
        copy.start()
    dests = out_ref.shape[0]
    blocks = y_ref.shape[0]
    half = blocks // 2
    base = 8 * half
    for copy in copies[1:]:
        copy.wait()
    fixed = jnp.bitwise_and(jnp.round(y_ref[...] * Y_SCALE).astype(I32), 0xFFFFFF)
    flags = jnp.bitwise_or(w_ref[...], lax.shift_left(b_ref[...], 16))
    lane = lax.broadcasted_iota(I32, (1, LANES), 1)
    nodes = jnp.zeros((1, LANES), I32)
    for k in range(blocks):
        nodes = jnp.where(lane == k, node_smem[k], nodes)
    last = fixed[11:12]
    top = lax.shift_left(lax.shift_right_logical(last, 16), 24)
    tail = jnp.concatenate(
        [
            fixed[0:3],
            jnp.bitwise_or(fixed[3:4], top),
            fixed[4:8],
            flags[8:12],
            fixed[8:11],
            jnp.bitwise_or(jnp.bitwise_and(last, 0xFFFF), lax.shift_left(nodes, 16)),
            flags[0:8],
        ],
        axis=0,
    )
    out_ref[:, pl.ds(base, TAIL), :] = jnp.broadcast_to(tail[None], (dests,) + tail.shape)
    copies[0].wait()
    for t in range(half):
        low = bins_ref[pl.ds(LANES * t, LANES), :]
        high = bins_ref[pl.ds(LANES * (t + half), LANES), :]
        packed = jnp.bitwise_or(low, lax.shift_left(high, 16)).T
        out_ref[:, pl.ds(8 * t, 8), :] = packed.reshape(dests, 8, LANES)


def split3(x):
    high = x.astype(BF16)
    rest = x - high.astype(F32)
    mid = rest.astype(BF16)
    low = (rest - mid.astype(F32)).astype(BF16)
    return high, mid, low


def hist_kernel(node_smem, recv_ref, sum_ref, cnt_ref, rho_ref, bag_ref, acc_ref, extra_smem, *, blocks):
    sources = recv_ref.shape[0]
    half = blocks // 2
    base = 8 * half
    rows = sources * SLOTS

    part_a, part_b, part_c = [recv_ref[:, pl.ds(base + 8 * p, 8), :] for p in range(3)]
    sub8 = lax.broadcasted_iota(I32, part_b.shape, 1)
    flags = jnp.concatenate([part_c, jnp.where(sub8 < 4, part_b, 0)], axis=1).reshape(rows, LANES)
    upper = pltpu.roll(part_b, 4, 1)
    mixed = jnp.bitwise_or(
        jnp.bitwise_and(upper, 0xFFFF),
        lax.shift_left(lax.shift_right_logical(part_a, 24), 16),
    )
    fixed = jnp.concatenate([part_a, jnp.where(sub8 == 3, mixed, upper)], axis=1)
    fixed = lax.shift_right_arithmetic(lax.shift_left(fixed, 8), 8)
    y = fixed.reshape(rows, LANES).astype(F32) * (1.0 / Y_SCALE)
    w = jnp.bitwise_and(flags, 0xFFFF).astype(F32)
    b = lax.shift_right_logical(flags, 16).astype(F32)
    sub = lax.broadcasted_iota(I32, (sources, SLOTS, LANES), 1)
    lane = lax.broadcasted_iota(I32, (sources, SLOTS, LANES), 2)
    node_row = lax.shift_right_logical(part_b[:, 7:8, :], 16).astype(F32)
    node_row = jnp.broadcast_to(node_row, (sources, SLOTS, LANES))
    node_col = jnp.sum(jnp.where(sub == lane, node_row, 0.0), axis=2, keepdims=True)
    node_col = node_col.reshape(rows, 1)
    lanes = lax.broadcasted_iota(I32, (rows, LANES), 1)
    wanted = jnp.where(lanes < 3 * NODES, jnp.bitwise_and(lanes, NODES - 1), -1).astype(F32)
    hot3 = (jnp.broadcast_to(node_col, (rows, LANES)) == wanted).astype(F32)
    hot_t = hot3.T.astype(BF16)[:NODES]
    bw = b * w
    stats = jnp.concatenate(
        [b.astype(BF16), bw.astype(BF16), *split3(b * y), *split3(bw * y)], axis=1
    )
    sums = jnp.dot(hot_t, stats, preferred_element_type=F32)

    def total(first_part, parts):
        out = sums[:, LANES * first_part : LANES * (first_part + 1)]
        for p in range(1, parts):
            out = out + sums[:, LANES * (first_part + p) : LANES * (first_part + p + 1)]
        return jnp.sum(out, axis=1, keepdims=True)

    count_n = total(0, 1)
    sum_w = total(1, 1)
    sum_y = total(2, 3)
    sum_wy = total(5, 3)
    shrunk = count_n + 1.0
    wbar = sum_w / shrunk
    ybar = sum_y / shrunk
    cov = sum_wy - wbar * sum_y - ybar * sum_w + count_n * wbar * ybar
    spread = sum_w - 2.0 * wbar * sum_w + count_n * wbar * wbar + 1.0
    effect = cov / spread
    scale = shrunk / spread
    params = jnp.concatenate(
        [jnp.broadcast_to(p, (NODES, LANES)) for p in (wbar, ybar, effect, scale)], axis=1
    )
    params = jnp.concatenate(
        [*split3(params), jnp.zeros((LANES - 3 * NODES, 4 * LANES), BF16)], axis=0
    )
    spread_out = jnp.dot(hot3.astype(BF16), params, preferred_element_type=F32)
    r_wbar, r_ybar, r_effect, r_scale = [
        spread_out[:, LANES * p : LANES * (p + 1)] for p in range(4)
    ]
    centred = w - r_wbar
    rho_ref[...] = b * centred * ((y - r_ybar) - centred * r_effect) * r_scale
    bag_ref[...] = b

    acc_ref[...] = jnp.zeros_like(acc_ref)
    iota_bin = lax.broadcasted_iota(I32, (16, LANES), 0).astype(I16)
    lane_group = lax.shift_right_logical(lax.broadcasted_iota(I32, (NODES, LANES), 1), 4)
    merge_group = lax.shift_right_logical(lax.broadcasted_iota(I32, (32, LANES), 1), 4)
    one = jnp.ones((16, LANES), BF16)
    zero = jnp.zeros((16, LANES), BF16)
    group = 4 if blocks % 4 == 0 else 1

    def group_sums(s, start, target):
        lefts, rights = [], []
        for n in range(group):
            k = start + n
            if isinstance(k, int):
                tile = recv_ref[s, pl.ds(8 * (k % half), 8), :]
                if k < half:
                    tile = jnp.bitwise_and(tile, 0xFFFF)
                else:
                    tile = lax.shift_right_logical(tile, 16)
            else:
                upper = (k >= half).astype(I32)
                tile = recv_ref[s, pl.ds(pl.multiple_of(8 * (k - half * upper), 8), 8), :]
                tile = jnp.bitwise_and(lax.shift_right_logical(tile, jnp.full(tile.shape, 16 * upper)), 0xFFFF)
            hi = lax.shift_right_logical(tile, 4)
            lo = jnp.bitwise_and(tile, 15)
            row = s * SLOTS + k
            keep = (node_smem[s, k] == target).astype(F32)
            rho = jnp.broadcast_to(rho_ref[pl.ds(row, 1), :] * keep, (16, LANES)).astype(BF16)
            bag = jnp.broadcast_to(bag_ref[pl.ds(row, 1), :] * keep, (16, LANES)).astype(BF16)
            left, right = [], []
            for f in range(8):
                hot = jnp.broadcast_to(hi[f : f + 1], (16, LANES)).astype(I16) == iota_bin
                left += [jnp.where(hot, rho, zero), jnp.where(hot, bag, zero)]
                hot = jnp.broadcast_to(lo[f : f + 1], (16, LANES)).astype(I16) == iota_bin
                right.append(jnp.where(hot, one, zero))
            lefts.append(jnp.concatenate(left, axis=0))
            rights.append(jnp.concatenate(right, axis=0))
        prod = lax.dot_general(
            jnp.concatenate(lefts, axis=1),
            jnp.concatenate(rights, axis=1),
            (((1,), (1,)), ((), ())),
            preferred_element_type=F32,
        )
        merged = prod[0:32]
        for f in range(1, 8):
            merged = jnp.where(merge_group == f, prod[32 * f : 32 * f + 32], merged)
        return merged

    def one_source(s, found):
        pending = []
        for start in range(0, blocks, group):
            pending.append((node_smem[s, start], group_sums(s, start, node_smem[s, start])))
            for k in range(start + 1, start + group):
                extra_smem[found] = (s * blocks + start) * 32 + node_smem[s, k]
                found = found + (node_smem[s, k] != node_smem[s, k - 1]).astype(I32)
        for target, merged in pending:
            acc_ref[target] += merged
        return found

    found = lax.fori_loop(0, sources, one_source, jnp.int32(0), unroll=16)

    batch = 8
    for n in range(batch - 1):
        extra_smem[found + n] = jnp.int32(NODES)

    def some_extras(e, carry):
        pending = []
        for n in range(batch):
            code = extra_smem[batch * e + n]
            target = jnp.bitwise_and(code, 31)
            place = lax.shift_right_logical(code, 5)
            start = lax.rem(place, blocks)
            pending.append((target, group_sums(lax.div(place, blocks), start, target)))
        for target, merged in pending:
            acc_ref[target] += merged
        return carry

    lax.fori_loop(0, lax.div(found + batch - 1, batch), some_extras, 0)

    for v, out_ref in enumerate((sum_ref, cnt_ref)):
        for c in range(2):
            pieces = [acc_ref[:NODES, 16 * v + 8 * c + g, :] for g in range(8)]
            for f in range(8):
                out = None
                for g in range(8):
                    shift = (16 * (g - f)) % LANES
                    moved = pltpu.roll(pieces[g], shift, 1) if shift else pieces[g]
                    out = moved if out is None else jnp.where(lane_group == g, moved, out)
                out_ref[f, :, pl.ds(LANES * c, LANES)] = out


def shards(bins, outcome, treatment, bag, block_node):
    blocks = block_node.shape[0]
    dests = lax.axis_size("dp")
    own = bins.shape[1] // dests
    base = 8 * (blocks // 2)
    height = base + TAIL
    packed = pl.pallas_call(
        pack_kernel,
        out_shape=jax.ShapeDtypeStruct((dests, height, LANES), I32),
        in_specs=[pl.BlockSpec(memory_space=pl.ANY)] * 5,
        out_specs=pl.BlockSpec(memory_space=pltpu.VMEM),
        scratch_shapes=[
            pltpu.VMEM(bins.shape, I32),
            pltpu.VMEM((blocks, LANES), F32),
            pltpu.VMEM((blocks, LANES), I32),
            pltpu.VMEM((blocks, LANES), I32),
            pltpu.SMEM((blocks,), I32),
            pltpu.SemaphoreType.DMA((5,)),
        ],
        compiler_params=pltpu.CompilerParams(vmem_limit_bytes=60 * 2**20),
        name="pack",
    )(
        bins,
        outcome.reshape(blocks, LANES),
        treatment.reshape(blocks, LANES),
        bag.reshape(blocks, LANES),
        block_node,
    )
    recv = lax.all_to_all(packed, "dp", 0, 0, tiled=True)
    nodes = lax.shift_right_logical(recv[:, base + 15, :blocks], 16)
    out = jax.ShapeDtypeStruct((own, NODES, BINS), F32)
    vmem = pl.BlockSpec(memory_space=pltpu.VMEM)
    return pl.pallas_call(
        functools.partial(hist_kernel, blocks=blocks),
        out_shape=(out, out),
        in_specs=[pl.BlockSpec(memory_space=pltpu.SMEM), vmem],
        out_specs=(vmem, vmem),
        scratch_shapes=[
            pltpu.VMEM((dests * SLOTS, LANES), F32),
            pltpu.VMEM((dests * SLOTS, LANES), F32),
            pltpu.VMEM((NODES + 1, 32, LANES), F32),
            pltpu.SMEM((dests * blocks,), I32),
        ],
        compiler_params=pltpu.CompilerParams(vmem_limit_bytes=32 * 2**20),
        name="hist",
    )(nodes, recv)


def solution(mesh):
    return jax.shard_map(
        shards,
        mesh=mesh,
        in_specs=(P("dp", None), P("dp"), P("dp"), P(("leaf", "dp")), P("dp")),
        out_specs=(P(("leaf", "dp"), None, None), P(("leaf", "dp"), None, None)),
        check_vma=False,
    )
```

```python
import functools

import jax
import jax.numpy as jnp
from jax import lax
from jax.experimental import pallas as pl
from jax.experimental.pallas import tpu as pltpu
from jax.sharding import PartitionSpec as P

BINS = 256
NODES = 16
LANES = 128
SLOTS = 16
F32 = jnp.float32
BF16 = jnp.bfloat16
I32 = jnp.int32
I16 = jnp.int16
Y_SCALE = float(2**20)
TAIL = 24


def pack_kernel(
    bins_hbm, y_hbm, w_hbm, b_hbm, node_hbm, out_ref, bins_ref, y_ref, w_ref, b_ref, node_smem, sems
):
    copies = [
        pltpu.make_async_copy(src, dst, sems.at[n])
        for n, (src, dst) in enumerate(
            (
                (bins_hbm, bins_ref),
                (y_hbm, y_ref),
                (w_hbm, w_ref),
                (b_hbm, b_ref),
                (node_hbm, node_smem),
            )
        )
    ]
    for copy in copies:
        copy.start()
    dests = out_ref.shape[0]
    blocks = y_ref.shape[0]
    half = blocks // 2
    base = 8 * half
    for copy in copies[1:]:
        copy.wait()
    fixed = jnp.bitwise_and(jnp.round(y_ref[...] * Y_SCALE).astype(I32), 0xFFFFFF)
    flags = jnp.bitwise_or(w_ref[...], lax.shift_left(b_ref[...], 16))
    lane = lax.broadcasted_iota(I32, (1, LANES), 1)
    nodes = jnp.zeros((1, LANES), I32)
    for k in range(blocks):
        nodes = jnp.where(lane == k, node_smem[k], nodes)
    last = fixed[11:12]
    top = lax.shift_left(lax.shift_right_logical(last, 16), 24)
    tail = jnp.concatenate(
        [
            fixed[0:3],
            jnp.bitwise_or(fixed[3:4], top),
            fixed[4:8],
            flags[8:12],
            fixed[8:11],
            jnp.bitwise_or(jnp.bitwise_and(last, 0xFFFF), lax.shift_left(nodes, 16)),
            flags[0:8],
        ],
        axis=0,
    )
    out_ref[:, pl.ds(base, TAIL), :] = jnp.broadcast_to(tail[None], (dests,) + tail.shape)
    copies[0].wait()
    for t in range(half):
        low = bins_ref[pl.ds(LANES * t, LANES), :]
        high = bins_ref[pl.ds(LANES * (t + half), LANES), :]
        packed = jnp.bitwise_or(low, lax.shift_left(high, 16)).T
        out_ref[:, pl.ds(8 * t, 8), :] = packed.reshape(dests, 8, LANES)


def split3(x):
    high = x.astype(BF16)
    rest = x - high.astype(F32)
    mid = rest.astype(BF16)
    low = (rest - mid.astype(F32)).astype(BF16)
    return high, mid, low


def hist_kernel(node_smem, recv_ref, sum_ref, cnt_ref, rho_ref, bag_ref, acc_ref, extra_smem, *, blocks):
    sources = recv_ref.shape[0]
    half = blocks // 2
    base = 8 * half
    rows = sources * SLOTS

    part_a, part_b, part_c = [recv_ref[:, pl.ds(base + 8 * p, 8), :] for p in range(3)]
    sub8 = lax.broadcasted_iota(I32, part_b.shape, 1)
    flags = jnp.concatenate([part_c, jnp.where(sub8 < 4, part_b, 0)], axis=1).reshape(rows, LANES)
    upper = pltpu.roll(part_b, 4, 1)
    mixed = jnp.bitwise_or(
        jnp.bitwise_and(upper, 0xFFFF),
        lax.shift_left(lax.shift_right_logical(part_a, 24), 16),
    )
    fixed = jnp.concatenate([part_a, jnp.where(sub8 == 3, mixed, upper)], axis=1)
    fixed = lax.shift_right_arithmetic(lax.shift_left(fixed, 8), 8)
    y = fixed.reshape(rows, LANES).astype(F32) * (1.0 / Y_SCALE)
    w = jnp.bitwise_and(flags, 0xFFFF).astype(F32)
    b = lax.shift_right_logical(flags, 16).astype(F32)
    sub = lax.broadcasted_iota(I32, (sources, SLOTS, LANES), 1)
    lane = lax.broadcasted_iota(I32, (sources, SLOTS, LANES), 2)
    node_row = lax.shift_right_logical(part_b[:, 7:8, :], 16).astype(F32)
    node_row = jnp.broadcast_to(node_row, (sources, SLOTS, LANES))
    node_col = jnp.sum(jnp.where(sub == lane, node_row, 0.0), axis=2, keepdims=True)
    node_col = node_col.reshape(rows, 1)
    lanes = lax.broadcasted_iota(I32, (rows, LANES), 1)
    wanted = jnp.where(lanes < 3 * NODES, jnp.bitwise_and(lanes, NODES - 1), -1).astype(F32)
    hot3 = (jnp.broadcast_to(node_col, (rows, LANES)) == wanted).astype(F32)
    hot_t = hot3.T.astype(BF16)[:NODES]
    bw = b * w
    stats = jnp.concatenate(
        [b.astype(BF16), bw.astype(BF16), *split3(b * y), *split3(bw * y)], axis=1
    )
    sums = jnp.dot(hot_t, stats, preferred_element_type=F32)

    def total(first_part, parts):
        out = sums[:, LANES * first_part : LANES * (first_part + 1)]
        for p in range(1, parts):
            out = out + sums[:, LANES * (first_part + p) : LANES * (first_part + p + 1)]
        return jnp.sum(out, axis=1, keepdims=True)

    count_n = total(0, 1)
    sum_w = total(1, 1)
    sum_y = total(2, 3)
    sum_wy = total(5, 3)
    shrunk = count_n + 1.0
    wbar = sum_w / shrunk
    ybar = sum_y / shrunk
    cov = sum_wy - wbar * sum_y - ybar * sum_w + count_n * wbar * ybar
    spread = sum_w - 2.0 * wbar * sum_w + count_n * wbar * wbar + 1.0
    effect = cov / spread
    scale = shrunk / spread
    params = jnp.concatenate(
        [jnp.broadcast_to(p, (NODES, LANES)) for p in (wbar, ybar, effect, scale)], axis=1
    )
    params = jnp.concatenate(
        [*split3(params), jnp.zeros((LANES - 3 * NODES, 4 * LANES), BF16)], axis=0
    )
    spread_out = jnp.dot(hot3.astype(BF16), params, preferred_element_type=F32)
    r_wbar, r_ybar, r_effect, r_scale = [
        spread_out[:, LANES * p : LANES * (p + 1)] for p in range(4)
    ]
    centred = w - r_wbar
    rho_ref[...] = b * centred * ((y - r_ybar) - centred * r_effect) * r_scale
    bag_ref[...] = b

    acc_ref[...] = jnp.zeros_like(acc_ref)
    iota_bin = lax.broadcasted_iota(I32, (16, LANES), 0).astype(I16)
    lane_group = lax.shift_right_logical(lax.broadcasted_iota(I32, (NODES, LANES), 1), 4)
    merge_group = lax.shift_right_logical(lax.broadcasted_iota(I32, (32, LANES), 1), 4)
    one = jnp.ones((16, LANES), BF16)
    zero = jnp.zeros((16, LANES), BF16)
    group = 2 if blocks % 2 == 0 else 1

    def group_sums(s, start, target, first_is_target=False):
        lefts, rights = [], []
        for n in range(group):
            k = start + n
            if isinstance(k, int):
                tile = recv_ref[s, pl.ds(8 * (k % half), 8), :]
                if k < half:
                    tile = jnp.bitwise_and(tile, 0xFFFF)
                else:
                    tile = lax.shift_right_logical(tile, 16)
            else:
                upper = (k >= half).astype(I32)
                tile = recv_ref[s, pl.ds(pl.multiple_of(8 * (k - half * upper), 8), 8), :]
                tile = jnp.bitwise_and(lax.shift_right_logical(tile, jnp.full(tile.shape, 16 * upper)), 0xFFFF)
            hi = lax.shift_right_logical(tile, 4)
            lo = jnp.bitwise_and(tile, 15)
            row = s * SLOTS + k
            rho = rho_ref[pl.ds(row, 1), :]
            bag = bag_ref[pl.ds(row, 1), :]
            if n > 0 or not first_is_target:
                keep = (node_smem[s, k] == target).astype(F32)
                rho, bag = rho * keep, bag * keep
            rho = jnp.broadcast_to(rho, (16, LANES)).astype(BF16)
            bag = jnp.broadcast_to(bag, (16, LANES)).astype(BF16)
            left, right = [], []
            for f in range(8):
                hot = jnp.broadcast_to(hi[f : f + 1], (16, LANES)).astype(I16) == iota_bin
                left += [jnp.where(hot, rho, zero), jnp.where(hot, bag, zero)]
                hot = jnp.broadcast_to(lo[f : f + 1], (16, LANES)).astype(I16) == iota_bin
                right.append(jnp.where(hot, one, zero))
            lefts.append(jnp.concatenate(left, axis=0))
            rights.append(jnp.concatenate(right, axis=0))
        prod = lax.dot_general(
            jnp.concatenate(lefts, axis=1),
            jnp.concatenate(rights, axis=1),
            (((1,), (1,)), ((), ())),
            preferred_element_type=F32,
        )
        merged = prod[0:32]
        for f in range(1, 8):
            merged = jnp.where(merge_group == f, prod[32 * f : 32 * f + 32], merged)
        return merged

    def one_source(s, found):
        pending = []
        for start in range(0, blocks, group):
            pending.append((node_smem[s, start], group_sums(s, start, node_smem[s, start], True)))
            for k in range(start + 1, start + group):
                extra_smem[found] = (s * blocks + start) * 32 + node_smem[s, k]
                found = found + (node_smem[s, k] != node_smem[s, k - 1]).astype(I32)
        for target, merged in pending:
            acc_ref[target] += merged
        return found

    found = lax.fori_loop(0, sources, one_source, jnp.int32(0), unroll=16)

    batch = 8
    for n in range(batch - 1):
        extra_smem[found + n] = jnp.int32(NODES)

    def some_extras(e, carry):
        pending = []
        for n in range(batch):
            code = extra_smem[batch * e + n]
            target = jnp.bitwise_and(code, 31)
            place = lax.shift_right_logical(code, 5)
            start = lax.rem(place, blocks)
            pending.append((target, group_sums(lax.div(place, blocks), start, target)))
        for target, merged in pending:
            acc_ref[target] += merged
        return carry

    lax.fori_loop(0, lax.div(found + batch - 1, batch), some_extras, 0)

    for v, out_ref in enumerate((sum_ref, cnt_ref)):
        for c in range(2):
            pieces = [acc_ref[:NODES, 16 * v + 8 * c + g, :] for g in range(8)]
            for f in range(8):
                out = None
                for g in range(8):
                    shift = (16 * (g - f)) % LANES
                    moved = pltpu.roll(pieces[g], shift, 1) if shift else pieces[g]
                    out = moved if out is None else jnp.where(lane_group == g, moved, out)
                out_ref[f, :, pl.ds(LANES * c, LANES)] = out


def shards(bins, outcome, treatment, bag, block_node):
    blocks = block_node.shape[0]
    dests = lax.axis_size("dp")
    own = bins.shape[1] // dests
    base = 8 * (blocks // 2)
    height = base + TAIL
    packed = pl.pallas_call(
        pack_kernel,
        out_shape=jax.ShapeDtypeStruct((dests, height, LANES), I32),
        in_specs=[pl.BlockSpec(memory_space=pl.ANY)] * 5,
        out_specs=pl.BlockSpec(memory_space=pltpu.VMEM),
        scratch_shapes=[
            pltpu.VMEM(bins.shape, I32),
            pltpu.VMEM((blocks, LANES), F32),
            pltpu.VMEM((blocks, LANES), I32),
            pltpu.VMEM((blocks, LANES), I32),
            pltpu.SMEM((blocks,), I32),
            pltpu.SemaphoreType.DMA((5,)),
        ],
        compiler_params=pltpu.CompilerParams(vmem_limit_bytes=60 * 2**20),
        name="pack",
    )(
        bins,
        outcome.reshape(blocks, LANES),
        treatment.reshape(blocks, LANES),
        bag.reshape(blocks, LANES),
        block_node,
    )
    recv = lax.all_to_all(packed, "dp", 0, 0, tiled=True)
    nodes = lax.shift_right_logical(recv[:, base + 15, :blocks], 16)
    out = jax.ShapeDtypeStruct((own, NODES, BINS), F32)
    vmem = pl.BlockSpec(memory_space=pltpu.VMEM)
    return pl.pallas_call(
        functools.partial(hist_kernel, blocks=blocks),
        out_shape=(out, out),
        in_specs=[pl.BlockSpec(memory_space=pltpu.SMEM), vmem],
        out_specs=(vmem, vmem),
        scratch_shapes=[
            pltpu.VMEM((dests * SLOTS, LANES), F32),
            pltpu.VMEM((dests * SLOTS, LANES), F32),
            pltpu.VMEM((NODES + 1, 32, LANES), F32),
            pltpu.SMEM((dests * blocks,), I32),
        ],
        compiler_params=pltpu.CompilerParams(vmem_limit_bytes=32 * 2**20),
        name="hist",
    )(nodes, recv)


def solution(mesh):
    return jax.shard_map(
        shards,
        mesh=mesh,
        in_specs=(P("dp", None), P("dp"), P("dp"), P(("leaf", "dp")), P("dp")),
        out_specs=(P(("leaf", "dp"), None, None), P(("leaf", "dp"), None, None)),
        check_vma=False,
    )
```
